32 devices in a mesh: urow: 8 (over z, core), icol: 4 (over y, x).
Axes of the slice: x: 2, y: 2, z: 4, core: 2. Of those that a mesh axis runs over, the one named last changes fastest.
Arguments:
- users: bfloat16 [8, 1024, 128], P('urow', 'icol'), may hold values from -6 to 6
- items: bfloat16 [1024, 4, 128], P('urow', 'icol'), may hold values from -6 to 6
- user_grad: bfloat16 [8, 1024, 128], P('urow', 'icol'), may hold values from -1.5 to 1.5
- item_grad: bfloat16 [1024, 4, 128], P('urow', 'icol'), may hold values from -1.5 to 1.5
- block_rows: int32 [8, 4, 12], P('urow', 'icol'), may hold values from 0 to 3, as said below
- block_cols: int32 [8, 4, 12], P('urow', 'icol'), may hold values from 0 to 3, as said below
- block_count: int32 [8, 4], P('urow', 'icol'), may hold values from 2 to 12, as said below
- block_values: bfloat16 [8, 4, 12, 256, 256], P('urow', 'icol'), may hold values from 0.0019989014 to 0.049804688
Outputs:
- user_next: bfloat16 [8, 1024, 128], P('urow', 'icol')
- item_next: bfloat16 [1024, 4, 128], P('urow', 'icol')
- user_back: bfloat16 [8, 1024, 128], P('urow', 'icol')
- item_back: bfloat16 [1024, 4, 128], P('urow', 'icol')
- value_grad: bfloat16 [8, 4, 12, 256, 256], P('urow', 'icol')
The draws below stay inside these ranges and needn't reach their ends.
Inputs may be any that keep to these rules, and one draw needn't show every extreme that they name: `block_rows`: within one tile the 12 slots name distinct (row, column) block pairs. `block_cols`: pairs with block_rows as stated there. `block_count`: some tile has all 12 slots live in every draw.
All inputs are finite; a program needn't handle non-finite values.
Results may differ from the reference program's by a relative error of at most 0.001.
Values may be sent and summed in bfloat16 or wider, within the bound.
A program may use at most 64 MiB of HBM per device.

```python
import math
import jax
import jax.numpy as jnp
from jax import lax

W = 128
BS = 256
UB = 4
IB = 4
MAXB = 12
N_UROW = 8
N_ICOL = 4


def tile_positions(key):
    tile_keys = jax.random.split(key, N_UROW * N_ICOL)
    shuffled = jax.vmap(lambda k: jax.random.permutation(k, UB * IB))(tile_keys)[:, :MAXB]
    return shuffled.reshape(N_UROW, N_ICOL, MAXB).astype(jnp.int32)


def draw_block_rows(key, part):
    placed = tile_positions(key)
    return (placed // IB).astype(jnp.int32)


def draw_block_cols(key, part):
    placed = tile_positions(key)
    return (placed % IB).astype(jnp.int32)


def draw_block_count(key, part):
    key = jax.random.fold_in(key, 3)
    first_key, second_key, third_key = jax.random.split(key, 3)
    lowest = max(1, MAXB // 6)
    highest = max(lowest + 1, MAXB // 3 + 1)
    base = jax.random.randint(first_key, (N_UROW, N_ICOL), lowest, highest, dtype=jnp.int32)
    filled = jax.random.randint(second_key, (N_UROW, N_ICOL), 0, 16, dtype=jnp.int32) == 0
    chosen = jax.random.randint(third_key, (), 0, N_UROW * N_ICOL, dtype=jnp.int32)
    filled = filled | (jnp.arange(N_UROW * N_ICOL, dtype=jnp.int32).reshape(N_UROW, N_ICOL) == chosen)
    return jnp.where(filled, MAXB, base).astype(jnp.int32)


def block_scale(key, extent, pieces, smallest, high):
    def one(axis_at, parts):
        heights = jax.random.uniform(jax.random.fold_in(jax.random.fold_in(key, 6), axis_at), (parts,), jnp.float32, smallest / len(pieces), high / len(pieces))
        return jnp.repeat(jnp.exp(heights), extent[axis_at] // parts).reshape((-1,) + (1,) * (len(extent) - axis_at - 1))

    level = one(*pieces[0])
    for cut in pieces[1:]:
        level = level * one(*cut)
    return level


def normal_values(rng, extent, deviation, limit, cuts=(), held_as=jnp.bfloat16):
    gain = block_scale(rng, extent, cuts, -0.22, 0.18) if cuts else 1.0
    result = jax.random.normal(rng, extent, jnp.float32) * deviation * gain
    return jnp.minimum(jnp.maximum(result, -limit), limit).astype(held_as)


def setup_inputs(seed: int = 0) -> dict:
    streams_of = jax.random.split(jax.random.key(seed), 9)
    users = normal_values(streams_of[0], (N_UROW, UB * BS, W), 1.0, 6.0, ((0, 8), (1, 4)))
    items = normal_values(streams_of[1], (IB * BS, N_ICOL, W), 1.0, 6.0, ((0, 8), (1, 4)))
    user_grad = normal_values(streams_of[2], (N_UROW, UB * BS, W), 0.25, 1.5, ((0, 8), (1, 4)))
    item_grad = normal_values(streams_of[3], (IB * BS, N_ICOL, W), 0.25, 1.5, ((0, 8), (1, 4)))
    block_rows = draw_block_rows(jax.random.fold_in(streams_of[8], 71), 0)
    block_cols = draw_block_cols(jax.random.fold_in(streams_of[8], 71), 0)
    block_count = draw_block_count(jax.random.fold_in(streams_of[8], 71), 0)
    block_values = jnp.clip(jnp.exp(math.log(0.049804688) - 3.2155114 * jax.random.uniform(streams_of[7], (N_UROW, N_ICOL, MAXB, BS, BS), jnp.float32) ** block_scale(streams_of[7], (N_UROW, N_ICOL, MAXB, BS, BS), ((0, 8), (1, 4)), -0.2, 0.2)), 0.0019989014, 0.049804688).astype(jnp.bfloat16)
    return dict(users=users, items=items, user_grad=user_grad, item_grad=item_grad, block_rows=block_rows, block_cols=block_cols, block_count=block_count, block_values=block_values)


def reference(users, items, user_grad, item_grad, block_rows, block_cols, block_count, block_values):
    highest = lax.Precision.HIGHEST

    def one_row(totals, row_at):
        user_pair = jnp.concatenate([users[row_at], user_grad[row_at]], 1).astype(jnp.float32).reshape(UB, BS, 2 * W)
        user_swap = jnp.concatenate([user_grad[row_at], users[row_at]], 1).astype(jnp.float32).reshape(UB, BS, 2 * W)

        def one_tile(col_at):
            item_pair = jnp.concatenate([items[:, col_at], item_grad[:, col_at]], 1).astype(jnp.float32).reshape(IB, BS, 2 * W)
            row_index = block_rows[row_at, col_at]
            col_index = block_cols[row_at, col_at]
            live_mask = jnp.arange(MAXB, dtype=jnp.int32) < block_count[row_at, col_at]
            masked = jnp.where(live_mask[:, None, None], block_values[row_at, col_at].astype(jnp.float32), 0.0)
            picked_items = item_pair[col_index]
            picked_users = user_pair[row_index]
            picked_swap = user_swap[row_index]
            user_blocks = jnp.einsum("kij,kjw->kiw", masked, picked_items, precision=highest)
            item_blocks = jnp.einsum("kij,kiw->kjw", masked, picked_users, precision=highest)
            row_hot = (row_index[:, None] == jnp.arange(UB, dtype=jnp.int32)[None, :]).astype(jnp.float32)
            col_hot = (col_index[:, None] == jnp.arange(IB, dtype=jnp.int32)[None, :]).astype(jnp.float32)
            user_part = jnp.einsum("ku,kiw->uiw", row_hot, user_blocks, precision=highest).reshape(UB * BS, 2 * W)
            item_part = jnp.einsum("ku,kiw->uiw", col_hot, item_blocks, precision=highest).reshape(IB * BS, 2 * W)
            grads = jnp.einsum("kiw,kjw->kij", picked_swap, picked_items, precision=highest)
            grads = jnp.where(live_mask[:, None, None], grads, 0.0).astype(jnp.bfloat16)
            return user_part, item_part, grads

        user_parts, item_parts, grads = lax.map(one_tile, jnp.arange(N_ICOL, dtype=jnp.int32))
        return totals + item_parts, (jnp.sum(user_parts, 0), grads)

    start_totals = jnp.zeros((N_ICOL, IB * BS, 2 * W), jnp.float32)
    item_totals, (user_totals, value_grad) = lax.scan(one_row, start_totals, jnp.arange(N_UROW, dtype=jnp.int32))
    user_next = user_totals[:, :, :W].astype(jnp.bfloat16)
    user_back = user_totals[:, :, W:].astype(jnp.bfloat16)
    item_next = jnp.transpose(item_totals[:, :, :W], (1, 0, 2)).astype(jnp.bfloat16)
    item_back = jnp.transpose(item_totals[:, :, W:], (1, 0, 2)).astype(jnp.bfloat16)
    return (user_next, item_next, user_back, item_back, value_grad)
```

```python
import functools

import jax
import jax.numpy as jnp
from jax import lax
from jax.experimental import pallas as pl
from jax.experimental.pallas import tpu as pltpu
from jax.sharding import PartitionSpec as P

MESH = pl.DeviceIdType.MESH


def kernel(
    n_urow, n_icol, users, items, user_grad, item_grad, rows, cols, count, values,
    user_next, item_next, user_back, item_back, grads_out,
    upair, ipair, blocks, dense, dense_t, upart, ipart, csum, pbuf, rbuf_i, rbuf_u, grads,
    local_sem, value_sem, grad_sem, su, ru, si, ri, sf, rf, sp, rp, sx, rx, sc, rc,
):
    width = users.shape[1]
    ru_rows, ri_rows = users.shape[0], items.shape[0]
    slots, size = values.shape[0], values.shape[1]
    ub, ib = upair.shape[0], ipair.shape[0]
    chips = n_urow // 2
    me_u, me_i = lax.axis_index("urow"), lax.axis_index("icol")
    core, chip = lax.rem(me_u, 2), me_u // 2
    partner = me_u + 1 - 2 * core

    def urows(index):
        return pl.ds(pl.multiple_of(index * ru_rows, ru_rows), ru_rows)

    def irows(index):
        return pl.ds(pl.multiple_of(index * ri_rows, ri_rows), ri_rows)

    def in_pair(index, count):
        start = index * count
        return start // size, pl.ds(pl.multiple_of(lax.rem(start, size), count), count)

    def upart_of(index):
        return upair.at[in_pair(index, ru_rows)]

    def ipart_of(index):
        return ipair.at[in_pair(index, ri_rows)]

    def remote(src, dst, send, recv, where):
        return pltpu.make_async_remote_copy(
            src_ref=src, dst_ref=dst, send_sem=send, recv_sem=recv,
            device_id=where, device_id_type=MESH,
        )

    chip_peers = [lax.rem(chip + o, chips) for o in range(1, chips)]
    icol_peers = [lax.rem(me_i + o, n_icol) for o in range(1, n_icol)]

    lo, hi = pl.ds(0, width), pl.ds(width, width)
    local = [
        pltpu.make_async_copy(items, ipair.at[(*in_pair(me_u, ri_rows), lo)], local_sem.at[0]),
        pltpu.make_async_copy(item_grad, ipair.at[(*in_pair(me_u, ri_rows), hi)], local_sem.at[1]),
        pltpu.make_async_copy(users, upair.at[(*in_pair(me_i, ru_rows), lo)], local_sem.at[2]),
        pltpu.make_async_copy(user_grad, upair.at[(*in_pair(me_i, ru_rows), hi)], local_sem.at[3]),
    ]
    for copy in local:
        copy.start()
    value_copy = pltpu.make_async_copy(values, blocks, value_sem)
    value_copy.start()

    barrier = pltpu.get_barrier_semaphore()
    pl.semaphore_signal(barrier, inc=1, device_id={"urow": partner}, device_id_type=MESH)
    for g in chip_peers:
        pl.semaphore_signal(barrier, inc=1, device_id={"urow": 2 * g + core}, device_id_type=MESH)
    for j in icol_peers:
        pl.semaphore_signal(barrier, inc=1, device_id={"icol": j}, device_id_type=MESH)
    pl.semaphore_wait(barrier, 1 + len(chip_peers) + len(icol_peers))
    for copy in local:
        copy.wait()

    mine_i, mine_u = ipart_of(me_u), upart_of(me_i)
    sends = []
    for g in chip_peers:
        sends.append(remote(mine_i, mine_i, si.at[g], ri.at[chip], {"urow": 2 * g + core}))
    for j in icol_peers:
        sends.append(remote(mine_u, mine_u, su.at[j], ru.at[me_i], {"icol": j}))
    sends.append(remote(mine_i, mine_i, sf.at[chip], rf.at[chip], {"urow": partner}))
    for copy in sends:
        copy.start()

    value_copy.wait()
    live_count = count[0, 0]
    for u in range(ub):
        for c in range(ib):
            slot, live = jnp.int32(0), jnp.float32(0.0)
            for k in range(slots):
                hit = (rows[0, 0, k] == u) & (cols[0, 0, k] == c) & (k < live_count)
                slot = jnp.where(hit, k, slot)
                live = jnp.where(hit, jnp.float32(1.0), live)
            block = (blocks[slot].astype(jnp.float32) * live).astype(jnp.bfloat16)
            dense[u * size:(u + 1) * size, c * size:(c + 1) * size] = block
            dense_t[c * size:(c + 1) * size, u * size:(u + 1) * size] = block.T

    for g in chip_peers:
        there = ipart_of(2 * g + core)
        remote(mine_i, there, si.at[g], ri.at[g], {"urow": partner}).wait_recv()
        copy = remote(there, there, sf.at[g], rf.at[g], {"urow": partner})
        copy.start()
        sends.append(copy)

    for j in icol_peers:
        remote(mine_u, upart_of(j), su.at[j], ru.at[j], {"icol": j}).wait_recv()
    for c in range(ib):
        at = slice(c * size, (c + 1) * size)
        ipart[at] = jnp.dot(dense_t[at], upair[...].reshape(-1, 2 * width), preferred_element_type=jnp.float32)
    for g in chip_peers + [chip]:
        copy = remote(
            ipart.at[irows(2 * g + 1 - core)], pbuf.at[g], sp.at[g], rp.at[g], {"urow": partner}
        )
        copy.start()
        sends.append(copy)

    for g in [chip] + chip_peers:
        there = ipart_of(2 * g + 1 - core)
        remote(there, there, sf.at[g], rf.at[g], {"urow": partner}).wait_recv()
    for u in range(ub):
        at = slice(u * size, (u + 1) * size)
        upart[at] = jnp.dot(dense[at], ipair[...].reshape(-1, 2 * width), preferred_element_type=jnp.float32)
    for j in icol_peers:
        copy = remote(upart.at[urows(j)], rbuf_u.at[me_i], sx.at[j], rx.at[me_i], {"icol": j})
        copy.start()
        sends.append(copy)

    for g in chip_peers + [chip]:
        remote(pbuf.at[g], pbuf.at[g], sp.at[g], rp.at[g], {"urow": partner}).wait_recv()
    for g in chip_peers:
        csum[g] = ipart[irows(2 * g + core)] + pbuf[g]
        copy = remote(csum.at[g], rbuf_i.at[chip], sc.at[g], rc.at[chip], {"urow": 2 * g + core})
        copy.start()
        sends.append(copy)

    writes = []
    for k in range(slots):
        left = upair[rows[0, 0, k]]
        right = ipair[cols[0, 0, k]]
        swap = jnp.concatenate([left[:, width:], left[:, :width]], 1)
        grad = lax.dot_general(
            swap, right, (((1,), (1,)), ((), ())), preferred_element_type=jnp.float32
        )
        grads[k] = jnp.where(k < live_count, grad, 0.0).astype(jnp.bfloat16)
        copy = pltpu.make_async_copy(grads.at[k], grads_out.at[k], grad_sem.at[k])
        copy.start()
        writes.append(copy)

    total = ipart[irows(me_u)] + pbuf[chip]
    for g in chip_peers:
        remote(csum.at[g], rbuf_i.at[g], sc.at[g], rc.at[g], {"urow": partner}).wait_recv()
        total = total + rbuf_i[g]
    item_next[...] = total[:, :width].astype(jnp.bfloat16)
    item_back[...] = total[:, width:].astype(jnp.bfloat16)
    total = upart[urows(me_i)]
    for j in icol_peers:
        remote(upart.at[urows(j)], rbuf_u.at[j], sx.at[j], rx.at[j], {"icol": j}).wait_recv()
        total = total + rbuf_u[j]
    user_next[...] = total[:, :width].astype(jnp.bfloat16)
    user_back[...] = total[:, width:].astype(jnp.bfloat16)
    for copy in writes:
        copy.wait()
    for copy in sends:
        copy.wait_send()


def shards(n_urow, n_icol, users, items, user_grad, item_grad, block_rows, block_cols, block_count, block_values):
    width = users.shape[2]
    ru_rows, ri_rows = users.shape[1], items.shape[0]
    slots, size = block_values.shape[2], block_values.shape[3]
    all_u, all_i = ru_rows * n_icol, ri_rows * n_urow
    chips = n_urow // 2
    bf16, f32 = jnp.bfloat16, jnp.float32
    hbm = pl.BlockSpec(memory_space=pl.ANY)
    smem = pl.BlockSpec(memory_space=pltpu.SMEM)
    vmem = pl.BlockSpec(memory_space=pltpu.VMEM)
    dma = pltpu.SemaphoreType.DMA
    un, in_, ub, ib, grads = pl.pallas_call(
        functools.partial(kernel, n_urow, n_icol),
        out_shape=(
            jax.ShapeDtypeStruct((ru_rows, width), bf16),
            jax.ShapeDtypeStruct((ri_rows, width), bf16),
            jax.ShapeDtypeStruct((ru_rows, width), bf16),
            jax.ShapeDtypeStruct((ri_rows, width), bf16),
            jax.ShapeDtypeStruct((slots, size, size), bf16),
        ),
        in_specs=[hbm] * 4 + [smem] * 3 + [hbm],
        out_specs=(vmem, vmem, vmem, vmem, hbm),
        scratch_shapes=[
            pltpu.VMEM((all_u // size, size, 2 * width), bf16),
            pltpu.VMEM((all_i // size, size, 2 * width), bf16),
            pltpu.VMEM((slots, size, size), bf16),
            pltpu.VMEM((all_u, all_i), bf16),
            pltpu.VMEM((all_i, all_u), bf16),
            pltpu.VMEM((all_u, 2 * width), f32),
            pltpu.VMEM((all_i, 2 * width), f32),
            pltpu.VMEM((chips, ri_rows, 2 * width), f32),
            pltpu.VMEM((chips, ri_rows, 2 * width), f32),
            pltpu.VMEM((chips, ri_rows, 2 * width), f32),
            pltpu.VMEM((n_icol, ru_rows, 2 * width), f32),
            pltpu.VMEM((slots, size, size), bf16),
            dma((4,)), dma, dma((slots,)),
            dma((n_icol,)), dma((n_icol,)), dma((chips,)), dma((chips,)),
            dma((chips,)), dma((chips,)), dma((chips,)), dma((chips,)),
            dma((n_icol,)), dma((n_icol,)), dma((chips,)), dma((chips,)),
        ],
        compiler_params=pltpu.CompilerParams(
            collective_id=0, has_side_effects=True, vmem_limit_bytes=63 * 1024 * 1024
        ),
    )(
        users.reshape(ru_rows, width), items.reshape(ri_rows, width),
        user_grad.reshape(ru_rows, width), item_grad.reshape(ri_rows, width),
        block_rows, block_cols, block_count, block_values.reshape(slots, size, size),
    )
    return (
        un.reshape(1, ru_rows, width), in_.reshape(ri_rows, 1, width),
        ub.reshape(1, ru_rows, width), ib.reshape(ri_rows, 1, width),
        grads.reshape(1, 1, slots, size, size),
    )


def solution(mesh):
    body = functools.partial(shards, mesh.shape["urow"], mesh.shape["icol"])
    row = P("urow", "icol", None)
    return jax.shard_map(
        body,
        mesh=mesh,
        in_specs=(row, row, row, row, row, row, P("urow", "icol"), P("urow", "icol", None, None, None)),
        out_specs=(row, row, row, row, P("urow", "icol", None, None, None)),
        check_vma=False,
    )
```

```python
import functools

import jax
import jax.numpy as jnp
from jax import lax
from jax.experimental import pallas as pl
from jax.experimental.pallas import tpu as pltpu
from jax.sharding import PartitionSpec as P

MESH = pl.DeviceIdType.MESH


LEVELS = 32766.0
STEPS = 88.0
EXTRA = 16


def encode(sums, coded):
    count = sums.shape[0]
    top = jnp.maximum(jnp.max(jnp.abs(sums), axis=0, keepdims=True), 1e-30)
    level = jnp.floor(jnp.log(top) * STEPS) + 2.0
    coded[:count] = jnp.round(sums * (jnp.exp(level * (-1.0 / STEPS)) * LEVELS)).astype(jnp.int32).astype(jnp.int16)
    level = jnp.broadcast_to(level, (EXTRA, sums.shape[1]))
    coded[count:] = level.astype(jnp.int32).astype(jnp.int16)


def decode(coded):
    count = coded.shape[0] - EXTRA
    level = coded[count:].astype(jnp.int32).astype(jnp.float32)[:1]
    return coded[:count].astype(jnp.int32).astype(jnp.float32) * (jnp.exp(level * (1.0 / STEPS)) * (1.0 / LEVELS))


def hand_over(*refs):
    half = (len(refs) - 1) // 2
    copies = [pltpu.make_async_copy(refs[i], refs[half + i], refs[-1].at[i]) for i in range(half)]
    for copy in copies:
        copy.start()
    for copy in copies:
        copy.wait()


def kernel(
    n_urow, n_icol, users, items, user_grad, item_grad, rows, cols, count, values,
    user_next, item_next, user_back, item_back, grads_out,
    upair, ipair, blocks, dense, dense_t, upart, ipart, csum, pbuf, sbuf_u, rbuf_i, rbuf_u, grads,
    local_sem, value_sem, grad_sem, su, ru, si, ri, sf, rf, sp, rp, sx, rx, sc, rc,
):
    width = users.shape[1]
    ru_rows, ri_rows = users.shape[0], items.shape[0]
    slots, size = values.shape[0], values.shape[1]
    ub, ib = upair.shape[0], ipair.shape[0]
    chips = n_urow // 2
    me_u, me_i = lax.axis_index("urow"), lax.axis_index("icol")
    core, chip = lax.rem(me_u, 2), me_u // 2
    partner = me_u + 1 - 2 * core

    def urows(index):
        return pl.ds(pl.multiple_of(index * ru_rows, ru_rows), ru_rows)

    def irows(index):
        return pl.ds(pl.multiple_of(index * ri_rows, ri_rows), ri_rows)

    def in_pair(index, count):
        start = index * count
        return start // size, pl.ds(pl.multiple_of(lax.rem(start, size), count), count)

    def upart_of(index):
        return upair.at[in_pair(index, ru_rows)]

    def ipart_of(index):
        return ipair.at[in_pair(index, ri_rows)]

    def remote(src, dst, send, recv, where):
        return pltpu.make_async_remote_copy(
            src_ref=src, dst_ref=dst, send_sem=send, recv_sem=recv,
            device_id=where, device_id_type=MESH,
        )

    chip_peers = [lax.rem(chip + o, chips) for o in range(1, chips)]
    icol_peers = [lax.rem(me_i + o, n_icol) for o in range(1, n_icol)]

    lo, hi = pl.ds(0, width), pl.ds(width, width)
    local = [
        pltpu.make_async_copy(items, ipair.at[(*in_pair(me_u, ri_rows), lo)], local_sem.at[0]),
        pltpu.make_async_copy(item_grad, ipair.at[(*in_pair(me_u, ri_rows), hi)], local_sem.at[1]),
        pltpu.make_async_copy(users, upair.at[(*in_pair(me_i, ru_rows), lo)], local_sem.at[2]),
        pltpu.make_async_copy(user_grad, upair.at[(*in_pair(me_i, ru_rows), hi)], local_sem.at[3]),
    ]
    for copy in local:
        copy.start()
    value_copy = pltpu.make_async_copy(values, blocks, value_sem)
    value_copy.start()

    barrier = pltpu.get_barrier_semaphore()
    pl.semaphore_signal(barrier, inc=1, device_id={"urow": partner}, device_id_type=MESH)
    for g in chip_peers:
        pl.semaphore_signal(barrier, inc=1, device_id={"urow": 2 * g + core}, device_id_type=MESH)
    for j in icol_peers:
        pl.semaphore_signal(barrier, inc=1, device_id={"icol": j}, device_id_type=MESH)
    pl.semaphore_wait(barrier, 1 + len(chip_peers) + len(icol_peers))
    for copy in local:
        copy.wait()

    mine_i, mine_u = ipart_of(me_u), upart_of(me_i)
    sends = []
    for g in chip_peers:
        sends.append(remote(mine_i, mine_i, si.at[g], ri.at[chip], {"urow": 2 * g + core}))
    for j in icol_peers:
        sends.append(remote(mine_u, mine_u, su.at[j], ru.at[me_i], {"icol": j}))
    sends.append(remote(mine_i, mine_i, sf.at[chip], rf.at[chip], {"urow": partner}))
    for copy in sends:
        copy.start()

    value_copy.wait()
    live_count = count[0, 0]
    for u in range(ub):
        for c in range(ib):
            slot, live = jnp.int32(0), jnp.float32(0.0)
            for k in range(slots):
                hit = (rows[0, 0, k] == u) & (cols[0, 0, k] == c) & (k < live_count)
                slot = jnp.where(hit, k, slot)
                live = jnp.where(hit, jnp.float32(1.0), live)
            block = (blocks[slot].astype(jnp.float32) * live).astype(jnp.bfloat16)
            dense[u * size:(u + 1) * size, c * size:(c + 1) * size] = block
            dense_t[c * size:(c + 1) * size, u * size:(u + 1) * size] = block.T

    for g in chip_peers:
        there = ipart_of(2 * g + core)
        remote(mine_i, there, si.at[g], ri.at[g], {"urow": partner}).wait_recv()
        copy = remote(there, there, sf.at[g], rf.at[g], {"urow": partner})
        copy.start()
        sends.append(copy)

    for j in icol_peers:
        remote(mine_u, upart_of(j), su.at[j], ru.at[j], {"icol": j}).wait_recv()
    for c in range(ib):
        at = slice(c * size, (c + 1) * size)
        ipart[at] = jnp.dot(dense_t[at], upair[...].reshape(-1, 2 * width), preferred_element_type=jnp.float32)
    for g in chip_peers + [chip]:
        copy = remote(
            ipart.at[irows(2 * g + 1 - core)], pbuf.at[g], sp.at[g], rp.at[g], {"urow": partner}
        )
        copy.start()
        sends.append(copy)

    for g in [chip] + chip_peers:
        there = ipart_of(2 * g + 1 - core)
        remote(there, there, sf.at[g], rf.at[g], {"urow": partner}).wait_recv()
    for u in range(ub):
        at = slice(u * size, (u + 1) * size)
        upart[at] = jnp.dot(dense[at], ipair[...].reshape(-1, 2 * width), preferred_element_type=jnp.float32)
    for j in icol_peers:
        encode(upart[urows(j)], sbuf_u.at[j])
        copy = remote(sbuf_u.at[j], rbuf_u.at[me_i], sx.at[j], rx.at[me_i], {"icol": j})
        copy.start()
        sends.append(copy)

    for g in chip_peers + [chip]:
        remote(pbuf.at[g], pbuf.at[g], sp.at[g], rp.at[g], {"urow": partner}).wait_recv()
    for g in chip_peers:
        encode(ipart[irows(2 * g + core)] + pbuf[g], csum.at[g])
        copy = remote(csum.at[g], rbuf_i.at[chip], sc.at[g], rc.at[chip], {"urow": 2 * g + core})
        copy.start()
        sends.append(copy)

    writes = []
    for k in range(slots):
        left = upair[rows[0, 0, k]]
        right = ipair[cols[0, 0, k]]
        swap = jnp.concatenate([left[:, width:], left[:, :width]], 1)
        grad = lax.dot_general(
            swap, right, (((1,), (1,)), ((), ())), preferred_element_type=jnp.float32
        )
        grads[k] = jnp.where(k < live_count, grad, 0.0).astype(jnp.bfloat16)
        copy = pltpu.make_async_copy(grads.at[k], grads_out.at[k], grad_sem.at[k])
        copy.start()
        writes.append(copy)

    total = ipart[irows(me_u)] + pbuf[chip]
    for g in chip_peers:
        remote(csum.at[g], rbuf_i.at[g], sc.at[g], rc.at[g], {"urow": partner}).wait_recv()
        total = total + decode(rbuf_i.at[g])
    item_next[...] = total[:, :width].astype(jnp.bfloat16)
    item_back[...] = total[:, width:].astype(jnp.bfloat16)
    total = upart[urows(me_i)]
    for j in icol_peers:
        remote(sbuf_u.at[j], rbuf_u.at[j], sx.at[j], rx.at[j], {"icol": j}).wait_recv()
        total = total + decode(rbuf_u.at[j])
    user_next[...] = total[:, :width].astype(jnp.bfloat16)
    user_back[...] = total[:, width:].astype(jnp.bfloat16)
    for copy in writes:
        copy.wait()
    for copy in sends:
        copy.wait_send()


def shards(n_urow, n_icol, users, items, user_grad, item_grad, block_rows, block_cols, block_count, block_values):
    width = users.shape[2]
    ru_rows, ri_rows = users.shape[1], items.shape[0]
    slots, size = block_values.shape[2], block_values.shape[3]
    all_u, all_i = ru_rows * n_icol, ri_rows * n_urow
    chips = n_urow // 2
    bf16, f32 = jnp.bfloat16, jnp.float32
    hbm = pl.BlockSpec(memory_space=pl.ANY)
    smem = pl.BlockSpec(memory_space=pltpu.SMEM)
    vmem = pl.BlockSpec(memory_space=pltpu.VMEM)
    dma = pltpu.SemaphoreType.DMA
    results = pl.pallas_call(
        functools.partial(kernel, n_urow, n_icol),
        out_shape=(
            jax.ShapeDtypeStruct((ru_rows, width), bf16),
            jax.ShapeDtypeStruct((ri_rows, width), bf16),
            jax.ShapeDtypeStruct((ru_rows, width), bf16),
            jax.ShapeDtypeStruct((ri_rows, width), bf16),
            jax.ShapeDtypeStruct((slots, size, size), bf16),
        ),
        in_specs=[hbm] * 4 + [smem] * 3 + [hbm],
        out_specs=(vmem, vmem, vmem, vmem, hbm),
        scratch_shapes=[
            pltpu.VMEM((all_u // size, size, 2 * width), bf16),
            pltpu.VMEM((all_i // size, size, 2 * width), bf16),
            pltpu.VMEM((slots, size, size), bf16),
            pltpu.VMEM((all_u, all_i), bf16),
            pltpu.VMEM((all_i, all_u), bf16),
            pltpu.VMEM((all_u, 2 * width), f32),
            pltpu.VMEM((all_i, 2 * width), f32),
            pltpu.VMEM((chips, ri_rows + EXTRA, 2 * width), jnp.int16),
            pltpu.VMEM((chips, ri_rows, 2 * width), f32),
            pltpu.VMEM((n_icol, ru_rows + EXTRA, 2 * width), jnp.int16),
            pltpu.VMEM((chips, ri_rows + EXTRA, 2 * width), jnp.int16),
            pltpu.VMEM((n_icol, ru_rows + EXTRA, 2 * width), jnp.int16),
            pltpu.VMEM((slots, size, size), bf16),
            dma((4,)), dma, dma((slots,)),
            dma((n_icol,)), dma((n_icol,)), dma((chips,)), dma((chips,)),
            dma((chips,)), dma((chips,)), dma((chips,)), dma((chips,)),
            dma((n_icol,)), dma((n_icol,)), dma((chips,)), dma((chips,)),
        ],
        compiler_params=pltpu.CompilerParams(
            collective_id=0, has_side_effects=True, vmem_limit_bytes=63 * 1024 * 1024
        ),
    )(
        users.reshape(ru_rows, width), items.reshape(ri_rows, width),
        user_grad.reshape(ru_rows, width), item_grad.reshape(ri_rows, width),
        block_rows, block_cols, block_count, block_values.reshape(slots, size, size),
    )
    un, in_, ub, ib, grads = pl.pallas_call(
        hand_over,
        out_shape=tuple(jax.ShapeDtypeStruct(r.shape, r.dtype) for r in results),
        in_specs=[hbm] * len(results),
        out_specs=(hbm,) * len(results),
        scratch_shapes=[dma((len(results),))],
        compiler_params=pltpu.CompilerParams(vmem_limit_bytes=63 * 1024 * 1024),
    )(*results)
    return (
        un.reshape(1, ru_rows, width), in_.reshape(ri_rows, 1, width),
        ub.reshape(1, ru_rows, width), ib.reshape(ri_rows, 1, width),
        grads.reshape(1, 1, slots, size, size),
    )


def solution(mesh):
    body = functools.partial(shards, mesh.shape["urow"], mesh.shape["icol"])
    row = P("urow", "icol", None)
    return jax.shard_map(
        body,
        mesh=mesh,
        in_specs=(row, row, row, row, row, row, P("urow", "icol"), P("urow", "icol", None, None, None)),
        out_specs=(row, row, row, row, P("urow", "icol", None, None, None)),
        check_vma=False,
    )
```

```python
import functools

import jax
import jax.numpy as jnp
from jax import lax
from jax.experimental import pallas as pl
from jax.experimental.pallas import tpu as pltpu
from jax.sharding import PartitionSpec as P

MESH = pl.DeviceIdType.MESH


LEVELS = 32766.0
STEPS = 88.0
EXTRA = 16


def encode(sums, coded):
    count = sums.shape[0]
    top = jnp.maximum(jnp.max(jnp.abs(sums), axis=0, keepdims=True), 1e-30)
    level = jnp.floor(jnp.log(top) * STEPS) + 2.0
    coded[:count] = jnp.round(sums * (jnp.exp(level * (-1.0 / STEPS)) * LEVELS)).astype(jnp.int32).astype(jnp.int16)
    level = jnp.broadcast_to(level, (EXTRA, sums.shape[1]))
    coded[count:] = level.astype(jnp.int32).astype(jnp.int16)


def decode(coded):
    count = coded.shape[0] - EXTRA
    level = coded[count:].astype(jnp.int32).astype(jnp.float32)[:1]
    return coded[:count].astype(jnp.int32).astype(jnp.float32) * (jnp.exp(level * (1.0 / STEPS)) * (1.0 / LEVELS))


def hand_over(*refs):
    given, taken, held, (in_sem, out_sem) = refs[:5], refs[5:10], refs[10:15], refs[15:]
    slots = given[4].shape[0]
    parts = [(given[i], held[i], taken[i]) for i in range(4)]
    parts += [(given[4].at[k], held[4].at[k], taken[4].at[k]) for k in range(slots)]
    loads = [pltpu.make_async_copy(p[0], p[1], in_sem.at[i]) for i, p in enumerate(parts)]
    stores = [pltpu.make_async_copy(p[1], p[2], out_sem.at[i]) for i, p in enumerate(parts)]
    for copy in loads:
        copy.start()
    for load, store in zip(loads, stores):
        load.wait()
        store.start()
    for copy in stores:
        copy.wait()


def kernel(
    n_urow, n_icol, users, items, user_grad, item_grad, rows, cols, count, values,
    user_next, item_next, user_back, item_back, grads_out,
    upair, ipair, blocks, dense, dense_t, upart, ipart, csum, pbuf, sbuf_u, rbuf_i, rbuf_u, grads,
    local_sem, value_sem, grad_sem, su, ru, si, ri, sf, rf, sp, rp, sx, rx, sc, rc,
):
    width = users.shape[1]
    ru_rows, ri_rows = users.shape[0], items.shape[0]
    slots, size = values.shape[0], values.shape[1]
    ub, ib = upair.shape[0], ipair.shape[0]
    chips = n_urow // 2
    me_u, me_i = lax.axis_index("urow"), lax.axis_index("icol")
    core, chip = lax.rem(me_u, 2), me_u // 2
    partner = me_u + 1 - 2 * core

    def urows(index):
        return pl.ds(pl.multiple_of(index * ru_rows, ru_rows), ru_rows)

    def irows(index):
        return pl.ds(pl.multiple_of(index * ri_rows, ri_rows), ri_rows)

    def in_pair(index, count):
        start = index * count
        return start // size, pl.ds(pl.multiple_of(lax.rem(start, size), count), count)

    def upart_of(index):
        return upair.at[in_pair(index, ru_rows)]

    def ipart_of(index):
        return ipair.at[in_pair(index, ri_rows)]

    def remote(src, dst, send, recv, where):
        return pltpu.make_async_remote_copy(
            src_ref=src, dst_ref=dst, send_sem=send, recv_sem=recv,
            device_id=where, device_id_type=MESH,
        )

    chip_peers = [lax.rem(chip + o, chips) for o in range(1, chips)]
    icol_peers = [lax.rem(me_i + o, n_icol) for o in range(1, n_icol)]

    lo, hi = pl.ds(0, width), pl.ds(width, width)
    local = [
        pltpu.make_async_copy(items, ipair.at[(*in_pair(me_u, ri_rows), lo)], local_sem.at[0]),
        pltpu.make_async_copy(item_grad, ipair.at[(*in_pair(me_u, ri_rows), hi)], local_sem.at[1]),
        pltpu.make_async_copy(users, upair.at[(*in_pair(me_i, ru_rows), lo)], local_sem.at[2]),
        pltpu.make_async_copy(user_grad, upair.at[(*in_pair(me_i, ru_rows), hi)], local_sem.at[3]),
    ]
    for copy in local:
        copy.start()
    value_copy = pltpu.make_async_copy(values, blocks, value_sem)
    value_copy.start()

    barrier = pltpu.get_barrier_semaphore()
    pl.semaphore_signal(barrier, inc=1, device_id={"urow": partner}, device_id_type=MESH)
    for g in chip_peers:
        pl.semaphore_signal(barrier, inc=1, device_id={"urow": 2 * g + core}, device_id_type=MESH)
    for j in icol_peers:
        pl.semaphore_signal(barrier, inc=1, device_id={"icol": j}, device_id_type=MESH)
    pl.semaphore_wait(barrier, 1 + len(chip_peers) + len(icol_peers))
    for copy in local:
        copy.wait()

    mine_i, mine_u = ipart_of(me_u), upart_of(me_i)
    sends = []
    for g in chip_peers:
        sends.append(remote(mine_i, mine_i, si.at[g], ri.at[chip], {"urow": 2 * g + core}))
    for j in icol_peers:
        sends.append(remote(mine_u, mine_u, su.at[j], ru.at[me_i], {"icol": j}))
    sends.append(remote(mine_i, mine_i, sf.at[chip], rf.at[chip], {"urow": partner}))
    for copy in sends:
        copy.start()

    value_copy.wait()
    live_count = count[0, 0]
    for u in range(ub):
        for c in range(ib):
            slot, live = jnp.int32(0), jnp.float32(0.0)
            for k in range(slots):
                hit = (rows[0, 0, k] == u) & (cols[0, 0, k] == c) & (k < live_count)
                slot = jnp.where(hit, k, slot)
                live = jnp.where(hit, jnp.float32(1.0), live)
            block = (blocks[slot].astype(jnp.float32) * live).astype(jnp.bfloat16)
            dense[u * size:(u + 1) * size, c * size:(c + 1) * size] = block
            dense_t[c * size:(c + 1) * size, u * size:(u + 1) * size] = block.T

    for g in chip_peers:
        there = ipart_of(2 * g + core)
        remote(mine_i, there, si.at[g], ri.at[g], {"urow": partner}).wait_recv()
        copy = remote(there, there, sf.at[g], rf.at[g], {"urow": partner})
        copy.start()
        sends.append(copy)

    for j in icol_peers:
        remote(mine_u, upart_of(j), su.at[j], ru.at[j], {"icol": j}).wait_recv()
    for c in range(ib):
        at = slice(c * size, (c + 1) * size)
        ipart[at] = jnp.dot(dense_t[at], upair[...].reshape(-1, 2 * width), preferred_element_type=jnp.float32)
    for g in chip_peers + [chip]:
        copy = remote(
            ipart.at[irows(2 * g + 1 - core)], pbuf.at[g], sp.at[g], rp.at[g], {"urow": partner}
        )
        copy.start()
        sends.append(copy)

    for g in [chip] + chip_peers:
        there = ipart_of(2 * g + 1 - core)
        remote(there, there, sf.at[g], rf.at[g], {"urow": partner}).wait_recv()
    for u in range(ub):
        at = slice(u * size, (u + 1) * size)
        upart[at] = jnp.dot(dense[at], ipair[...].reshape(-1, 2 * width), preferred_element_type=jnp.float32)
    for j in icol_peers:
        encode(upart[urows(j)], sbuf_u.at[j])
        copy = remote(sbuf_u.at[j], rbuf_u.at[me_i], sx.at[j], rx.at[me_i], {"icol": j})
        copy.start()
        sends.append(copy)

    for g in chip_peers + [chip]:
        remote(pbuf.at[g], pbuf.at[g], sp.at[g], rp.at[g], {"urow": partner}).wait_recv()
    for g in chip_peers:
        encode(ipart[irows(2 * g + core)] + pbuf[g], csum.at[g])
        copy = remote(csum.at[g], rbuf_i.at[chip], sc.at[g], rc.at[chip], {"urow": 2 * g + core})
        copy.start()
        sends.append(copy)

    writes = []
    for k in range(slots):
        left = upair[rows[0, 0, k]]
        right = ipair[cols[0, 0, k]]
        swap = jnp.concatenate([left[:, width:], left[:, :width]], 1)
        grad = lax.dot_general(
            swap, right, (((1,), (1,)), ((), ())), preferred_element_type=jnp.float32
        )
        grads[k] = jnp.where(k < live_count, grad, 0.0).astype(jnp.bfloat16)
        copy = pltpu.make_async_copy(grads.at[k], grads_out.at[k], grad_sem.at[k])
        copy.start()
        writes.append(copy)

    total = ipart[irows(me_u)] + pbuf[chip]
    for g in chip_peers:
        remote(csum.at[g], rbuf_i.at[g], sc.at[g], rc.at[g], {"urow": partner}).wait_recv()
        total = total + decode(rbuf_i.at[g])
    item_next[...] = total[:, :width].astype(jnp.bfloat16)
    item_back[...] = total[:, width:].astype(jnp.bfloat16)
    total = upart[urows(me_i)]
    for j in icol_peers:
        remote(sbuf_u.at[j], rbuf_u.at[j], sx.at[j], rx.at[j], {"icol": j}).wait_recv()
        total = total + decode(rbuf_u.at[j])
    user_next[...] = total[:, :width].astype(jnp.bfloat16)
    user_back[...] = total[:, width:].astype(jnp.bfloat16)
    for copy in writes:
        copy.wait()
    for copy in sends:
        copy.wait_send()


def shards(n_urow, n_icol, users, items, user_grad, item_grad, block_rows, block_cols, block_count, block_values):
    width = users.shape[2]
    ru_rows, ri_rows = users.shape[1], items.shape[0]
    slots, size = block_values.shape[2], block_values.shape[3]
    all_u, all_i = ru_rows * n_icol, ri_rows * n_urow
    chips = n_urow // 2
    bf16, f32 = jnp.bfloat16, jnp.float32
    hbm = pl.BlockSpec(memory_space=pl.ANY)
    smem = pl.BlockSpec(memory_space=pltpu.SMEM)
    vmem = pl.BlockSpec(memory_space=pltpu.VMEM)
    dma = pltpu.SemaphoreType.DMA
    results = pl.pallas_call(
        functools.partial(kernel, n_urow, n_icol),
        out_shape=(
            jax.ShapeDtypeStruct((ru_rows, width), bf16),
            jax.ShapeDtypeStruct((ri_rows, width), bf16),
            jax.ShapeDtypeStruct((ru_rows, width), bf16),
            jax.ShapeDtypeStruct((ri_rows, width), bf16),
            jax.ShapeDtypeStruct((slots, size, size), bf16),
        ),
        in_specs=[hbm] * 4 + [smem] * 3 + [hbm],
        out_specs=(vmem, vmem, vmem, vmem, hbm),
        scratch_shapes=[
            pltpu.VMEM((all_u // size, size, 2 * width), bf16),
            pltpu.VMEM((all_i // size, size, 2 * width), bf16),
            pltpu.VMEM((slots, size, size), bf16),
            pltpu.VMEM((all_u, all_i), bf16),
            pltpu.VMEM((all_i, all_u), bf16),
            pltpu.VMEM((all_u, 2 * width), f32),
            pltpu.VMEM((all_i, 2 * width), f32),
            pltpu.VMEM((chips, ri_rows + EXTRA, 2 * width), jnp.int16),
            pltpu.VMEM((chips, ri_rows, 2 * width), f32),
            pltpu.VMEM((n_icol, ru_rows + EXTRA, 2 * width), jnp.int16),
            pltpu.VMEM((chips, ri_rows + EXTRA, 2 * width), jnp.int16),
            pltpu.VMEM((n_icol, ru_rows + EXTRA, 2 * width), jnp.int16),
            pltpu.VMEM((slots, size, size), bf16),
            dma((4,)), dma, dma((slots,)),
            dma((n_icol,)), dma((n_icol,)), dma((chips,)), dma((chips,)),
            dma((chips,)), dma((chips,)), dma((chips,)), dma((chips,)),
            dma((n_icol,)), dma((n_icol,)), dma((chips,)), dma((chips,)),
        ],
        compiler_params=pltpu.CompilerParams(
            collective_id=0, has_side_effects=True, vmem_limit_bytes=63 * 1024 * 1024
        ),
    )(
        users.reshape(ru_rows, width), items.reshape(ri_rows, width),
        user_grad.reshape(ru_rows, width), item_grad.reshape(ri_rows, width),
        block_rows, block_cols, block_count, block_values.reshape(slots, size, size),
    )
    un, in_, ub, ib, grads = pl.pallas_call(
        hand_over,
        out_shape=tuple(jax.ShapeDtypeStruct(r.shape, r.dtype) for r in results),
        in_specs=[hbm] * len(results),
        out_specs=(hbm,) * len(results),
        scratch_shapes=[pltpu.VMEM(r.shape, r.dtype) for r in results] + [dma((slots + 4,)), dma((slots + 4,))],
        compiler_params=pltpu.CompilerParams(vmem_limit_bytes=63 * 1024 * 1024),
    )(*results)
    return (
        un.reshape(1, ru_rows, width), in_.reshape(ri_rows, 1, width),
        ub.reshape(1, ru_rows, width), ib.reshape(ri_rows, 1, width),
        grads.reshape(1, 1, slots, size, size),
    )


def solution(mesh):
    body = functools.partial(shards, mesh.shape["urow"], mesh.shape["icol"])
    row = P("urow", "icol", None)
    return jax.shard_map(
        body,
        mesh=mesh,
        in_specs=(row, row, row, row, row, row, P("urow", "icol"), P("urow", "icol", None, None, None)),
        out_specs=(row, row, row, row, P("urow", "icol", None, None, None)),
        check_vma=False,
    )
```

```python
import functools

import jax
import jax.numpy as jnp
from jax import lax
from jax.experimental import pallas as pl
from jax.experimental.pallas import tpu as pltpu
from jax.sharding import PartitionSpec as P

MESH = pl.DeviceIdType.MESH


LEVELS = 32766.0
STEPS = 88.0
EXTRA = 16


def encode(sums, coded):
    count = sums.shape[0]
    top = jnp.maximum(jnp.max(jnp.abs(sums), axis=0, keepdims=True), 1e-30)
    level = jnp.floor(jnp.log(top) * STEPS) + 2.0
    coded[:count] = jnp.round(sums * (jnp.exp(level * (-1.0 / STEPS)) * LEVELS)).astype(jnp.int32).astype(jnp.int16)
    level = jnp.broadcast_to(level, (EXTRA, sums.shape[1]))
    coded[count:] = level.astype(jnp.int32).astype(jnp.int16)


def decode(coded):
    count = coded.shape[0] - EXTRA
    level = coded[count:].astype(jnp.int32).astype(jnp.float32)[:1]
    return coded[:count].astype(jnp.int32).astype(jnp.float32) * (jnp.exp(level * (1.0 / STEPS)) * (1.0 / LEVELS))


def hand_over(*refs):
    given, taken, sem = refs[:5], refs[5:10], refs[10]
    copies = [pltpu.make_async_copy(given[i], taken[i], sem.at[i]) for i in range(5)]
    for copy in copies:
        copy.start()
    for copy in copies:
        copy.wait()


def kernel(
    n_urow, n_icol, users, items, user_grad, item_grad, rows_in, cols_in, count_in, values,
    user_next, item_next, user_back, item_back, grads,
    upair, ipair, blocks, dense, dense_t, upart, ipart, csum, pbuf, sbuf_u, rbuf_i, rbuf_u, rows, cols, count,
    local_sem, value_sem, index_sem, su, ru, si, ri, sf, rf, sp, rp, sx, rx, sc, rc,
):
    width = users.shape[1]
    ru_rows, ri_rows = users.shape[0], items.shape[0]
    slots, size = values.shape[0], values.shape[1]
    ub, ib = upair.shape[0], ipair.shape[0]
    chips = n_urow // 2
    me_u, me_i = lax.axis_index("urow"), lax.axis_index("icol")
    core, chip = lax.rem(me_u, 2), me_u // 2
    partner = me_u + 1 - 2 * core

    def urows(index):
        return pl.ds(pl.multiple_of(index * ru_rows, ru_rows), ru_rows)

    def irows(index):
        return pl.ds(pl.multiple_of(index * ri_rows, ri_rows), ri_rows)

    def in_pair(index, count):
        start = index * count
        return start // size, pl.ds(pl.multiple_of(lax.rem(start, size), count), count)

    def upart_of(index):
        return upair.at[in_pair(index, ru_rows)]

    def ipart_of(index):
        return ipair.at[in_pair(index, ri_rows)]

    def remote(src, dst, send, recv, where):
        return pltpu.make_async_remote_copy(
            src_ref=src, dst_ref=dst, send_sem=send, recv_sem=recv,
            device_id=where, device_id_type=MESH,
        )

    chip_peers = [lax.rem(chip + o, chips) for o in range(1, chips)]
    icol_peers = [lax.rem(me_i + o, n_icol) for o in range(1, n_icol)]

    barrier = pltpu.get_barrier_semaphore()
    pl.semaphore_signal(barrier, inc=1, device_id={"urow": partner}, device_id_type=MESH)
    for g in chip_peers:
        pl.semaphore_signal(barrier, inc=1, device_id={"urow": 2 * g + core}, device_id_type=MESH)
    for j in icol_peers:
        pl.semaphore_signal(barrier, inc=1, device_id={"icol": j}, device_id_type=MESH)

    lo, hi = pl.ds(0, width), pl.ds(width, width)
    local = [
        pltpu.make_async_copy(items, ipair.at[(*in_pair(me_u, ri_rows), lo)], local_sem.at[0]),
        pltpu.make_async_copy(item_grad, ipair.at[(*in_pair(me_u, ri_rows), hi)], local_sem.at[1]),
        pltpu.make_async_copy(users, upair.at[(*in_pair(me_i, ru_rows), lo)], local_sem.at[2]),
        pltpu.make_async_copy(user_grad, upair.at[(*in_pair(me_i, ru_rows), hi)], local_sem.at[3]),
    ]
    for copy in local:
        copy.start()
    value_copy = pltpu.make_async_copy(values, blocks, value_sem)
    value_copy.start()
    index_copies = [
        pltpu.make_async_copy(src, dst, index_sem.at[i])
        for i, (src, dst) in enumerate([(rows_in, rows), (cols_in, cols), (count_in, count)])
    ]
    for copy in index_copies:
        copy.start()
    pl.semaphore_wait(barrier, 1 + len(chip_peers) + len(icol_peers))
    for copy in local:
        copy.wait()

    mine_i, mine_u = ipart_of(me_u), upart_of(me_i)
    sends = []
    for g in chip_peers:
        sends.append(remote(mine_i, mine_i, si.at[g], ri.at[chip], {"urow": 2 * g + core}))
    for j in icol_peers:
        sends.append(remote(mine_u, mine_u, su.at[j], ru.at[me_i], {"icol": j}))
    sends.append(remote(mine_i, mine_i, sf.at[chip], rf.at[chip], {"urow": partner}))
    for copy in sends:
        copy.start()

    for copy in index_copies:
        copy.wait()
    value_copy.wait()
    live_count = count[0, 0]
    for u in range(ub):
        for c in range(ib):
            slot, live = jnp.int32(0), jnp.float32(0.0)
            for k in range(slots):
                hit = (rows[0, 0, k] == u) & (cols[0, 0, k] == c) & (k < live_count)
                slot = jnp.where(hit, k, slot)
                live = jnp.where(hit, jnp.float32(1.0), live)
            block = (blocks[slot].astype(jnp.float32) * live).astype(jnp.bfloat16)
            dense[u * size:(u + 1) * size, c * size:(c + 1) * size] = block
            dense_t[c * size:(c + 1) * size, u * size:(u + 1) * size] = block.T

    for g in chip_peers:
        there = ipart_of(2 * g + core)
        remote(mine_i, there, si.at[g], ri.at[g], {"urow": partner}).wait_recv()
        copy = remote(there, there, sf.at[g], rf.at[g], {"urow": partner})
        copy.start()
        sends.append(copy)

    for j in icol_peers:
        remote(mine_u, upart_of(j), su.at[j], ru.at[j], {"icol": j}).wait_recv()
    for c in range(ib):
        at = slice(c * size, (c + 1) * size)
        ipart[at] = jnp.dot(dense_t[at], upair[...].reshape(-1, 2 * width), preferred_element_type=jnp.float32)
    for g in chip_peers + [chip]:
        copy = remote(
            ipart.at[irows(2 * g + 1 - core)], pbuf.at[g], sp.at[g], rp.at[g], {"urow": partner}
        )
        copy.start()
        sends.append(copy)

    for g in [chip] + chip_peers:
        there = ipart_of(2 * g + 1 - core)
        remote(there, there, sf.at[g], rf.at[g], {"urow": partner}).wait_recv()
    for u in range(ub):
        at = slice(u * size, (u + 1) * size)
        upart[at] = jnp.dot(dense[at], ipair[...].reshape(-1, 2 * width), preferred_element_type=jnp.float32)
    for j in icol_peers:
        encode(upart[urows(j)], sbuf_u.at[j])
        copy = remote(sbuf_u.at[j], rbuf_u.at[me_i], sx.at[j], rx.at[me_i], {"icol": j})
        copy.start()
        sends.append(copy)

    for g in chip_peers + [chip]:
        remote(pbuf.at[g], pbuf.at[g], sp.at[g], rp.at[g], {"urow": partner}).wait_recv()
    for g in chip_peers:
        encode(ipart[irows(2 * g + core)] + pbuf[g], csum.at[g])
        copy = remote(csum.at[g], rbuf_i.at[chip], sc.at[g], rc.at[chip], {"urow": 2 * g + core})
        copy.start()
        sends.append(copy)

    for k in range(slots):
        left = upair[rows[0, 0, k]]
        right = ipair[cols[0, 0, k]]
        swap = jnp.concatenate([left[:, width:], left[:, :width]], 1)
        grad = lax.dot_general(
            swap, right, (((1,), (1,)), ((), ())), preferred_element_type=jnp.float32
        )
        grads[k] = jnp.where(k < live_count, grad, 0.0).astype(jnp.bfloat16)

    total = ipart[irows(me_u)] + pbuf[chip]
    for g in chip_peers:
        remote(csum.at[g], rbuf_i.at[g], sc.at[g], rc.at[g], {"urow": partner}).wait_recv()
        total = total + decode(rbuf_i.at[g])
    item_next[...] = total[:, :width].astype(jnp.bfloat16)
    item_back[...] = total[:, width:].astype(jnp.bfloat16)
    total = upart[urows(me_i)]
    for j in icol_peers:
        remote(sbuf_u.at[j], rbuf_u.at[j], sx.at[j], rx.at[j], {"icol": j}).wait_recv()
        total = total + decode(rbuf_u.at[j])
    user_next[...] = total[:, :width].astype(jnp.bfloat16)
    user_back[...] = total[:, width:].astype(jnp.bfloat16)
    for copy in sends:
        copy.wait_send()


def shards(n_urow, n_icol, users, items, user_grad, item_grad, block_rows, block_cols, block_count, block_values):
    width = users.shape[2]
    ru_rows, ri_rows = users.shape[1], items.shape[0]
    slots, size = block_values.shape[2], block_values.shape[3]
    all_u, all_i = ru_rows * n_icol, ri_rows * n_urow
    chips = n_urow // 2
    bf16, f32 = jnp.bfloat16, jnp.float32
    hbm = pl.BlockSpec(memory_space=pltpu.HBM)
    vmem = pl.BlockSpec(memory_space=pltpu.VMEM)
    dma = pltpu.SemaphoreType.DMA
    results = pl.pallas_call(
        functools.partial(kernel, n_urow, n_icol),
        out_shape=(
            pltpu.VMEM((ru_rows, width), bf16),
            pltpu.VMEM((ri_rows, width), bf16),
            pltpu.VMEM((ru_rows, width), bf16),
            pltpu.VMEM((ri_rows, width), bf16),
            pltpu.VMEM((slots, size, size), bf16),
        ),
        in_specs=[hbm] * 8,
        out_specs=(vmem,) * 5,
        scratch_shapes=[
            pltpu.VMEM((all_u // size, size, 2 * width), bf16),
            pltpu.VMEM((all_i // size, size, 2 * width), bf16),
            pltpu.VMEM((slots, size, size), bf16),
            pltpu.VMEM((all_u, all_i), bf16),
            pltpu.VMEM((all_i, all_u), bf16),
            pltpu.VMEM((all_u, 2 * width), f32),
            pltpu.VMEM((all_i, 2 * width), f32),
            pltpu.VMEM((chips, ri_rows + EXTRA, 2 * width), jnp.int16),
            pltpu.VMEM((chips, ri_rows, 2 * width), f32),
            pltpu.VMEM((n_icol, ru_rows + EXTRA, 2 * width), jnp.int16),
            pltpu.VMEM((chips, ri_rows + EXTRA, 2 * width), jnp.int16),
            pltpu.VMEM((n_icol, ru_rows + EXTRA, 2 * width), jnp.int16),
            pltpu.SMEM(block_rows.shape, jnp.int32), pltpu.SMEM(block_cols.shape, jnp.int32),
            pltpu.SMEM(block_count.shape, jnp.int32),
            dma((4,)), dma, dma((3,)),
            dma((n_icol,)), dma((n_icol,)), dma((chips,)), dma((chips,)),
            dma((chips,)), dma((chips,)), dma((chips,)), dma((chips,)),
            dma((n_icol,)), dma((n_icol,)), dma((chips,)), dma((chips,)),
        ],
        compiler_params=pltpu.CompilerParams(
            collective_id=0, has_side_effects=True, vmem_limit_bytes=62 * 1024 * 1024
        ),
    )(
        users.reshape(ru_rows, width), items.reshape(ri_rows, width),
        user_grad.reshape(ru_rows, width), item_grad.reshape(ri_rows, width),
        block_rows, block_cols, block_count, block_values.reshape(slots, size, size),
    )
    un, in_, ub, ib, grads = pl.pallas_call(
        hand_over,
        out_shape=tuple(jax.ShapeDtypeStruct(r.shape, r.dtype) for r in results),
        in_specs=[vmem] * len(results),
        out_specs=(hbm,) * len(results),
        scratch_shapes=[dma((len(results),))],
    )(*results)
    return (
        un.reshape(1, ru_rows, width), in_.reshape(ri_rows, 1, width),
        ub.reshape(1, ru_rows, width), ib.reshape(ri_rows, 1, width),
        grads.reshape(1, 1, slots, size, size),
    )


def solution(mesh):
    body = functools.partial(shards, mesh.shape["urow"], mesh.shape["icol"])
    row = P("urow", "icol", None)
    return jax.shard_map(
        body,
        mesh=mesh,
        in_specs=(row, row, row, row, row, row, P("urow", "icol"), P("urow", "icol", None, None, None)),
        out_specs=(row, row, row, row, P("urow", "icol", None, None, None)),
        check_vma=False,
    )
```

```python
import functools

import jax
import jax.numpy as jnp
from jax import lax
from jax.experimental import pallas as pl
from jax.experimental.pallas import tpu as pltpu
from jax.sharding import PartitionSpec as P

MESH = pl.DeviceIdType.MESH


LEVELS = 32766.0
STEPS = 88.0
EXTRA = 16


def encode(sums, coded):
    count = sums.shape[0]
    top = jnp.maximum(jnp.max(jnp.abs(sums), axis=0, keepdims=True), 1e-30)
    level = jnp.floor(jnp.log(top) * STEPS) + 2.0
    coded[:count] = jnp.round(sums * (jnp.exp(level * (-1.0 / STEPS)) * LEVELS)).astype(jnp.int32).astype(jnp.int16)
    level = jnp.broadcast_to(level, (EXTRA, sums.shape[1]))
    coded[count:] = level.astype(jnp.int32).astype(jnp.int16)


def decode(coded):
    count = coded.shape[0] - EXTRA
    level = coded[count:].astype(jnp.int32).astype(jnp.float32)[:1]
    return coded[:count].astype(jnp.int32).astype(jnp.float32) * (jnp.exp(level * (1.0 / STEPS)) * (1.0 / LEVELS))


def hand_over(*refs):
    given, taken, sem = refs[:5], refs[5:10], refs[10]
    copies = [pltpu.make_async_copy(given[i], taken[i], sem.at[i]) for i in range(5)]
    for copy in copies:
        copy.start()
    for copy in copies:
        copy.wait()


def kernel(
    n_urow, n_icol, users, items, user_grad, item_grad, rows_in, cols_in, count, values,
    user_next, item_next, user_back, item_back, grads,
    upair, ipair, blocks, dense, dense_t, upart, ipart, csum, pbuf, sbuf_u, rbuf_i, rbuf_u, rows, cols,
    local_sem, value_sem, index_sem, su, ru, si, ri, sf, rf, sp, rp, sx, rx, sc, rc,
):
    width = users.shape[1]
    ru_rows, ri_rows = users.shape[0], items.shape[0]
    slots, size = values.shape[0], values.shape[1]
    ub, ib = upair.shape[0], ipair.shape[0]
    chips = n_urow // 2
    me_u, me_i = lax.axis_index("urow"), lax.axis_index("icol")
    core, chip = lax.rem(me_u, 2), me_u // 2
    partner = me_u + 1 - 2 * core

    def urows(index):
        return pl.ds(pl.multiple_of(index * ru_rows, ru_rows), ru_rows)

    def irows(index):
        return pl.ds(pl.multiple_of(index * ri_rows, ri_rows), ri_rows)

    def in_pair(index, count):
        start = index * count
        return start // size, pl.ds(pl.multiple_of(lax.rem(start, size), count), count)

    def upart_of(index):
        return upair.at[in_pair(index, ru_rows)]

    def ipart_of(index):
        return ipair.at[in_pair(index, ri_rows)]

    def remote(src, dst, send, recv, where):
        return pltpu.make_async_remote_copy(
            src_ref=src, dst_ref=dst, send_sem=send, recv_sem=recv,
            device_id=where, device_id_type=MESH,
        )

    chip_peers = [lax.rem(chip + o, chips) for o in range(1, chips)]
    icol_peers = [lax.rem(me_i + o, n_icol) for o in range(1, n_icol)]

    barrier = pltpu.get_barrier_semaphore()
    pl.semaphore_signal(barrier, inc=1, device_id={"urow": partner}, device_id_type=MESH)
    for g in chip_peers:
        pl.semaphore_signal(barrier, inc=1, device_id={"urow": 2 * g + core}, device_id_type=MESH)
    for j in icol_peers:
        pl.semaphore_signal(barrier, inc=1, device_id={"icol": j}, device_id_type=MESH)

    lo, hi = pl.ds(0, width), pl.ds(width, width)
    local = [
        pltpu.make_async_copy(items, ipair.at[(*in_pair(me_u, ri_rows), lo)], local_sem.at[0]),
        pltpu.make_async_copy(item_grad, ipair.at[(*in_pair(me_u, ri_rows), hi)], local_sem.at[1]),
        pltpu.make_async_copy(users, upair.at[(*in_pair(me_i, ru_rows), lo)], local_sem.at[2]),
        pltpu.make_async_copy(user_grad, upair.at[(*in_pair(me_i, ru_rows), hi)], local_sem.at[3]),
    ]
    for copy in local:
        copy.start()
    value_copy = pltpu.make_async_copy(values, blocks, value_sem)
    value_copy.start()
    index_copies = [
        pltpu.make_async_copy(src, dst, index_sem.at[i])
        for i, (src, dst) in enumerate([(rows_in, rows), (cols_in, cols)])
    ]
    for copy in index_copies:
        copy.start()
    pl.semaphore_wait(barrier, 1 + len(chip_peers) + len(icol_peers))
    for copy in local:
        copy.wait()

    mine_i, mine_u = ipart_of(me_u), upart_of(me_i)
    sends = []
    for g in chip_peers:
        sends.append(remote(mine_i, mine_i, si.at[g], ri.at[chip], {"urow": 2 * g + core}))
    for j in icol_peers:
        sends.append(remote(mine_u, mine_u, su.at[j], ru.at[me_i], {"icol": j}))
    sends.append(remote(mine_i, mine_i, sf.at[chip], rf.at[chip], {"urow": partner}))
    for copy in sends:
        copy.start()

    for copy in index_copies:
        copy.wait()
    value_copy.wait()
    live_count = count[0, 0]
    for u in range(ub):
        for c in range(ib):
            slot, live = jnp.int32(0), jnp.float32(0.0)
            for k in range(slots):
                hit = (rows[0, 0, k] == u) & (cols[0, 0, k] == c) & (k < live_count)
                slot = jnp.where(hit, k, slot)
                live = jnp.where(hit, jnp.float32(1.0), live)
            block = (blocks[slot].astype(jnp.float32) * live).astype(jnp.bfloat16)
            dense[u * size:(u + 1) * size, c * size:(c + 1) * size] = block
            dense_t[c * size:(c + 1) * size, u * size:(u + 1) * size] = block.T

    for g in chip_peers:
        there = ipart_of(2 * g + core)
        remote(mine_i, there, si.at[g], ri.at[g], {"urow": partner}).wait_recv()
        copy = remote(there, there, sf.at[g], rf.at[g], {"urow": partner})
        copy.start()
        sends.append(copy)

    for j in icol_peers:
        remote(mine_u, upart_of(j), su.at[j], ru.at[j], {"icol": j}).wait_recv()
    for c in range(ib):
        at = slice(c * size, (c + 1) * size)
        ipart[at] = jnp.dot(dense_t[at], upair[...].reshape(-1, 2 * width), preferred_element_type=jnp.float32)
    for g in chip_peers + [chip]:
        copy = remote(
            ipart.at[irows(2 * g + 1 - core)], pbuf.at[g], sp.at[g], rp.at[g], {"urow": partner}
        )
        copy.start()
        sends.append(copy)

    for g in [chip] + chip_peers:
        there = ipart_of(2 * g + 1 - core)
        remote(there, there, sf.at[g], rf.at[g], {"urow": partner}).wait_recv()
    for u in range(ub):
        at = slice(u * size, (u + 1) * size)
        upart[at] = jnp.dot(dense[at], ipair[...].reshape(-1, 2 * width), preferred_element_type=jnp.float32)
    for j in icol_peers:
        encode(upart[urows(j)], sbuf_u.at[j])
        copy = remote(sbuf_u.at[j], rbuf_u.at[me_i], sx.at[j], rx.at[me_i], {"icol": j})
        copy.start()
        sends.append(copy)

    for g in chip_peers + [chip]:
        remote(pbuf.at[g], pbuf.at[g], sp.at[g], rp.at[g], {"urow": partner}).wait_recv()
    for g in chip_peers:
        encode(ipart[irows(2 * g + core)] + pbuf[g], csum.at[g])
        copy = remote(csum.at[g], rbuf_i.at[chip], sc.at[g], rc.at[chip], {"urow": 2 * g + core})
        copy.start()
        sends.append(copy)

    for k in range(slots):
        left = upair[rows[0, 0, k]]
        right = ipair[cols[0, 0, k]]
        swap = jnp.concatenate([left[:, width:], left[:, :width]], 1)
        grad = lax.dot_general(
            swap, right, (((1,), (1,)), ((), ())), preferred_element_type=jnp.float32
        )
        grads[k] = jnp.where(k < live_count, grad, 0.0).astype(jnp.bfloat16)

    total = ipart[irows(me_u)] + pbuf[chip]
    for g in chip_peers:
        remote(csum.at[g], rbuf_i.at[g], sc.at[g], rc.at[g], {"urow": partner}).wait_recv()
        total = total + decode(rbuf_i.at[g])
    item_next[...] = total[:, :width].astype(jnp.bfloat16)
    item_back[...] = total[:, width:].astype(jnp.bfloat16)
    total = upart[urows(me_i)]
    for j in icol_peers:
        remote(sbuf_u.at[j], rbuf_u.at[j], sx.at[j], rx.at[j], {"icol": j}).wait_recv()
        total = total + decode(rbuf_u.at[j])
    user_next[...] = total[:, :width].astype(jnp.bfloat16)
    user_back[...] = total[:, width:].astype(jnp.bfloat16)
    for copy in sends:
        copy.wait_send()


def shards(n_urow, n_icol, users, items, user_grad, item_grad, block_rows, block_cols, block_count, block_values):
    width = users.shape[2]
    ru_rows, ri_rows = users.shape[1], items.shape[0]
    slots, size = block_values.shape[2], block_values.shape[3]
    all_u, all_i = ru_rows * n_icol, ri_rows * n_urow
    chips = n_urow // 2
    bf16, f32 = jnp.bfloat16, jnp.float32
    hbm = pl.BlockSpec(memory_space=pltpu.HBM)
    vmem = pl.BlockSpec(memory_space=pltpu.VMEM)
    dma = pltpu.SemaphoreType.DMA
    results = pl.pallas_call(
        functools.partial(kernel, n_urow, n_icol),
        out_shape=(
            pltpu.VMEM((ru_rows, width), bf16),
            pltpu.VMEM((ri_rows, width), bf16),
            pltpu.VMEM((ru_rows, width), bf16),
            pltpu.VMEM((ri_rows, width), bf16),
            pltpu.VMEM((slots, size, size), bf16),
        ),
        in_specs=[hbm] * 6 + [pl.BlockSpec(memory_space=pltpu.SMEM), hbm],
        out_specs=(vmem,) * 5,
        scratch_shapes=[
            pltpu.VMEM((all_u // size, size, 2 * width), bf16),
            pltpu.VMEM((all_i // size, size, 2 * width), bf16),
            pltpu.VMEM((slots, size, size), bf16),
            pltpu.VMEM((all_u, all_i), bf16),
            pltpu.VMEM((all_i, all_u), bf16),
            pltpu.VMEM((all_u, 2 * width), f32),
            pltpu.VMEM((all_i, 2 * width), f32),
            pltpu.VMEM((chips, ri_rows + EXTRA, 2 * width), jnp.int16),
            pltpu.VMEM((chips, ri_rows, 2 * width), f32),
            pltpu.VMEM((n_icol, ru_rows + EXTRA, 2 * width), jnp.int16),
            pltpu.VMEM((chips, ri_rows + EXTRA, 2 * width), jnp.int16),
            pltpu.VMEM((n_icol, ru_rows + EXTRA, 2 * width), jnp.int16),
            pltpu.SMEM(block_rows.shape, jnp.int32), pltpu.SMEM(block_cols.shape, jnp.int32),
            dma((4,)), dma, dma((2,)),
            dma((n_icol,)), dma((n_icol,)), dma((chips,)), dma((chips,)),
            dma((chips,)), dma((chips,)), dma((chips,)), dma((chips,)),
            dma((n_icol,)), dma((n_icol,)), dma((chips,)), dma((chips,)),
        ],
        compiler_params=pltpu.CompilerParams(
            collective_id=0, has_side_effects=True, vmem_limit_bytes=62 * 1024 * 1024
        ),
    )(
        users.reshape(ru_rows, width), items.reshape(ri_rows, width),
        user_grad.reshape(ru_rows, width), item_grad.reshape(ri_rows, width),
        block_rows, block_cols, block_count, block_values.reshape(slots, size, size),
    )
    un, in_, ub, ib, grads = pl.pallas_call(
        hand_over,
        out_shape=tuple(jax.ShapeDtypeStruct(r.shape, r.dtype) for r in results),
        in_specs=[vmem] * len(results),
        out_specs=(hbm,) * len(results),
        scratch_shapes=[dma((len(results),))],
        compiler_params=pltpu.CompilerParams(vmem_limit_bytes=1024 * 1024),
    )(*results)
    return (
        un.reshape(1, ru_rows, width), in_.reshape(ri_rows, 1, width),
        ub.reshape(1, ru_rows, width), ib.reshape(ri_rows, 1, width),
        grads.reshape(1, 1, slots, size, size),
    )


def solution(mesh):
    body = functools.partial(shards, mesh.shape["urow"], mesh.shape["icol"])
    row = P("urow", "icol", None)
    return jax.shard_map(
        body,
        mesh=mesh,
        in_specs=(row, row, row, row, row, row, P("urow", "icol"), P("urow", "icol", None, None, None)),
        out_specs=(row, row, row, row, P("urow", "icol", None, None, None)),
        check_vma=False,
    )
```

```python
import functools

import jax
import jax.numpy as jnp
from jax import lax
from jax.experimental import pallas as pl
from jax.experimental.pallas import tpu as pltpu
from jax.sharding import PartitionSpec as P

MESH = pl.DeviceIdType.MESH


LEVELS = 32766.0
STEPS = 88.0
EXTRA = 16


def encode(sums, coded):
    count = sums.shape[0]
    top = jnp.maximum(jnp.max(jnp.abs(sums), axis=0, keepdims=True), 1e-30)
    level = jnp.floor(jnp.log(top) * STEPS) + 2.0
    coded[:count] = jnp.round(sums * (jnp.exp(level * (-1.0 / STEPS)) * LEVELS)).astype(jnp.int32).astype(jnp.int16)
    level = jnp.broadcast_to(level, (EXTRA, sums.shape[1]))
    coded[count:] = level.astype(jnp.int32).astype(jnp.int16)


def decode(coded):
    count = coded.shape[0] - EXTRA
    level = coded[count:].astype(jnp.int32).astype(jnp.float32)[:1]
    return coded[:count].astype(jnp.int32).astype(jnp.float32) * (jnp.exp(level * (1.0 / STEPS)) * (1.0 / LEVELS))


def hand_over(*refs):
    given, taken, sem = refs[:5], refs[5:10], refs[10]
    copies = [pltpu.make_async_copy(given[i], taken[i], sem.at[i]) for i in range(5)]
    for copy in copies:
        copy.start()
    for copy in copies:
        copy.wait()


def kernel(
    n_urow, n_icol, users, items, user_grad, item_grad, rows_in, cols_in, count, values,
    user_next, item_next, user_back, item_back, grads,
    upair, ipair, blocks, dense, dense_t, upart, ipart, csum, pbuf, sbuf_u, rbuf_i, rbuf_u, rows, cols,
    local_sem, value_sem, index_sem, su, ru, si, ri, sf, rf, sp, rp, sx, rx, sc, rc,
):
    width = users.shape[1]
    ru_rows, ri_rows = users.shape[0], items.shape[0]
    slots, size = values.shape[0], values.shape[1]
    ub, ib = upair.shape[0], ipair.shape[0]
    chips = n_urow // 2
    me_u, me_i = lax.axis_index("urow"), lax.axis_index("icol")
    core, chip = lax.rem(me_u, 2), me_u // 2
    partner = me_u + 1 - 2 * core

    def urows(index):
        return pl.ds(pl.multiple_of(index * ru_rows, ru_rows), ru_rows)

    def irows(index):
        return pl.ds(pl.multiple_of(index * ri_rows, ri_rows), ri_rows)

    def in_pair(index, count):
        start = index * count
        return start // size, pl.ds(pl.multiple_of(lax.rem(start, size), count), count)

    def upart_of(index):
        return upair.at[in_pair(index, ru_rows)]

    def ipart_of(index):
        return ipair.at[in_pair(index, ri_rows)]

    def remote(src, dst, send, recv, where):
        return pltpu.make_async_remote_copy(
            src_ref=src, dst_ref=dst, send_sem=send, recv_sem=recv,
            device_id=where, device_id_type=MESH,
        )

    chip_peers = [lax.rem(chip + o, chips) for o in range(1, chips)]
    icol_peers = [lax.rem(me_i + o, n_icol) for o in range(1, n_icol)]

    barrier = pltpu.get_barrier_semaphore()
    pl.semaphore_signal(barrier, inc=1, device_id={"urow": partner}, device_id_type=MESH)
    for g in chip_peers:
        pl.semaphore_signal(barrier, inc=1, device_id={"urow": 2 * g + core}, device_id_type=MESH)
    for j in icol_peers:
        pl.semaphore_signal(barrier, inc=1, device_id={"icol": j}, device_id_type=MESH)

    lo, hi = pl.ds(0, width), pl.ds(width, width)
    local = [
        pltpu.make_async_copy(items, ipair.at[(*in_pair(me_u, ri_rows), lo)], local_sem.at[0]),
        pltpu.make_async_copy(item_grad, ipair.at[(*in_pair(me_u, ri_rows), hi)], local_sem.at[1]),
        pltpu.make_async_copy(users, upair.at[(*in_pair(me_i, ru_rows), lo)], local_sem.at[2]),
        pltpu.make_async_copy(user_grad, upair.at[(*in_pair(me_i, ru_rows), hi)], local_sem.at[3]),
    ]
    for copy in local:
        copy.start()
    value_copy = pltpu.make_async_copy(values, blocks, value_sem)
    value_copy.start()
    index_copies = [
        pltpu.make_async_copy(src, dst, index_sem.at[i])
        for i, (src, dst) in enumerate([(rows_in, rows), (cols_in, cols)])
    ]
    for copy in index_copies:
        copy.start()
    pl.semaphore_wait(barrier, 1 + len(chip_peers) + len(icol_peers))
    for copy in local:
        copy.wait()

    mine_i, mine_u = ipart_of(me_u), upart_of(me_i)
    sends = []
    for g in chip_peers:
        sends.append(remote(mine_i, mine_i, si.at[g], ri.at[chip], {"urow": 2 * g + core}))
    for j in icol_peers:
        sends.append(remote(mine_u, mine_u, su.at[j], ru.at[me_i], {"icol": j}))
    sends.append(remote(mine_i, mine_i, sf.at[chip], rf.at[chip], {"urow": partner}))
    for copy in sends:
        copy.start()

    for copy in index_copies:
        copy.wait()
    value_copy.wait()
    live_count = count[0, 0]
    for u in range(ub):
        for c in range(ib):
            slot, live = jnp.int32(0), jnp.float32(0.0)
            for k in range(slots):
                hit = (rows[0, 0, k] == u) & (cols[0, 0, k] == c) & (k < live_count)
                slot = jnp.where(hit, k, slot)
                live = jnp.where(hit, jnp.float32(1.0), live)
            block = (blocks[slot].astype(jnp.float32) * live).astype(jnp.bfloat16)
            dense[u * size:(u + 1) * size, c * size:(c + 1) * size] = block
            dense_t[c * size:(c + 1) * size, u * size:(u + 1) * size] = block.T

    for g in chip_peers:
        there = ipart_of(2 * g + core)
        remote(mine_i, there, si.at[g], ri.at[g], {"urow": partner}).wait_recv()
        copy = remote(there, there, sf.at[g], rf.at[g], {"urow": partner})
        copy.start()
        sends.append(copy)

    for j in icol_peers:
        remote(mine_u, upart_of(j), su.at[j], ru.at[j], {"icol": j}).wait_recv()
    for g in chip_peers + [chip]:
        at = pl.ds(pl.multiple_of(g * 2 * ri_rows, 2 * ri_rows), 2 * ri_rows)
        ipart[at] = jnp.dot(
            dense_t[at], upair[...].reshape(-1, 2 * width), preferred_element_type=jnp.float32
        )
        copy = remote(
            ipart.at[irows(2 * g + 1 - core)], pbuf.at[g], sp.at[g], rp.at[g], {"urow": partner}
        )
        copy.start()
        sends.append(copy)

    for g in [chip] + chip_peers:
        there = ipart_of(2 * g + 1 - core)
        remote(there, there, sf.at[g], rf.at[g], {"urow": partner}).wait_recv()

    def user_sums(j):
        return jnp.dot(
            dense[urows(j)], ipair[...].reshape(-1, 2 * width), preferred_element_type=jnp.float32
        )

    for o in range(max(len(icol_peers), len(chip_peers))):
        if o < len(icol_peers):
            j = icol_peers[o]
            encode(user_sums(j), sbuf_u.at[j])
            copy = remote(sbuf_u.at[j], rbuf_u.at[me_i], sx.at[j], rx.at[me_i], {"icol": j})
            copy.start()
            sends.append(copy)
        if o < len(chip_peers):
            g = chip_peers[o]
            remote(pbuf.at[g], pbuf.at[g], sp.at[g], rp.at[g], {"urow": partner}).wait_recv()
            encode(ipart[irows(2 * g + core)] + pbuf[g], csum.at[g])
            copy = remote(csum.at[g], rbuf_i.at[chip], sc.at[g], rc.at[chip], {"urow": 2 * g + core})
            copy.start()
            sends.append(copy)
    remote(pbuf.at[chip], pbuf.at[chip], sp.at[chip], rp.at[chip], {"urow": partner}).wait_recv()
    upart[...] = user_sums(me_i)

    for k in range(slots):
        left = upair[rows[0, 0, k]]
        right = ipair[cols[0, 0, k]]
        swap = jnp.concatenate([left[:, width:], left[:, :width]], 1)
        grad = lax.dot_general(
            swap, right, (((1,), (1,)), ((), ())), preferred_element_type=jnp.float32
        )
        grads[k] = jnp.where(k < live_count, grad, 0.0).astype(jnp.bfloat16)

    total = ipart[irows(me_u)] + pbuf[chip]
    for g in chip_peers:
        remote(csum.at[g], rbuf_i.at[g], sc.at[g], rc.at[g], {"urow": partner}).wait_recv()
        total = total + decode(rbuf_i.at[g])
    item_next[...] = total[:, :width].astype(jnp.bfloat16)
    item_back[...] = total[:, width:].astype(jnp.bfloat16)
    total = upart[...]
    for j in icol_peers:
        remote(sbuf_u.at[j], rbuf_u.at[j], sx.at[j], rx.at[j], {"icol": j}).wait_recv()
        total = total + decode(rbuf_u.at[j])
    user_next[...] = total[:, :width].astype(jnp.bfloat16)
    user_back[...] = total[:, width:].astype(jnp.bfloat16)
    for copy in sends:
        copy.wait_send()


def shards(n_urow, n_icol, users, items, user_grad, item_grad, block_rows, block_cols, block_count, block_values):
    width = users.shape[2]
    ru_rows, ri_rows = users.shape[1], items.shape[0]
    slots, size = block_values.shape[2], block_values.shape[3]
    all_u, all_i = ru_rows * n_icol, ri_rows * n_urow
    chips = n_urow // 2
    bf16, f32 = jnp.bfloat16, jnp.float32
    hbm = pl.BlockSpec(memory_space=pltpu.HBM)
    vmem = pl.BlockSpec(memory_space=pltpu.VMEM)
    dma = pltpu.SemaphoreType.DMA
    results = pl.pallas_call(
        functools.partial(kernel, n_urow, n_icol),
        out_shape=(
            pltpu.VMEM((ru_rows, width), bf16),
            pltpu.VMEM((ri_rows, width), bf16),
            pltpu.VMEM((ru_rows, width), bf16),
            pltpu.VMEM((ri_rows, width), bf16),
            pltpu.VMEM((slots, size, size), bf16),
        ),
        in_specs=[hbm] * 6 + [pl.BlockSpec(memory_space=pltpu.SMEM), hbm],
        out_specs=(vmem,) * 5,
        scratch_shapes=[
            pltpu.VMEM((all_u // size, size, 2 * width), bf16),
            pltpu.VMEM((all_i // size, size, 2 * width), bf16),
            pltpu.VMEM((slots, size, size), bf16),
            pltpu.VMEM((all_u, all_i), bf16),
            pltpu.VMEM((all_i, all_u), bf16),
            pltpu.VMEM((ru_rows, 2 * width), f32),
            pltpu.VMEM((all_i, 2 * width), f32),
            pltpu.VMEM((chips, ri_rows + EXTRA, 2 * width), jnp.int16),
            pltpu.VMEM((chips, ri_rows, 2 * width), f32),
            pltpu.VMEM((n_icol, ru_rows + EXTRA, 2 * width), jnp.int16),
            pltpu.VMEM((chips, ri_rows + EXTRA, 2 * width), jnp.int16),
            pltpu.VMEM((n_icol, ru_rows + EXTRA, 2 * width), jnp.int16),
            pltpu.SMEM(block_rows.shape, jnp.int32), pltpu.SMEM(block_cols.shape, jnp.int32),
            dma((4,)), dma, dma((2,)),
            dma((n_icol,)), dma((n_icol,)), dma((chips,)), dma((chips,)),
            dma((chips,)), dma((chips,)), dma((chips,)), dma((chips,)),
            dma((n_icol,)), dma((n_icol,)), dma((chips,)), dma((chips,)),
        ],
        compiler_params=pltpu.CompilerParams(
            collective_id=0, has_side_effects=True, vmem_limit_bytes=62 * 1024 * 1024
        ),
    )(
        users.reshape(ru_rows, width), items.reshape(ri_rows, width),
        user_grad.reshape(ru_rows, width), item_grad.reshape(ri_rows, width),
        block_rows, block_cols, block_count, block_values.reshape(slots, size, size),
    )
    un, in_, ub, ib, grads = pl.pallas_call(
        hand_over,
        out_shape=tuple(jax.ShapeDtypeStruct(r.shape, r.dtype) for r in results),
        in_specs=[vmem] * len(results),
        out_specs=(hbm,) * len(results),
        scratch_shapes=[dma((len(results),))],
        compiler_params=pltpu.CompilerParams(vmem_limit_bytes=1024 * 1024),
    )(*results)
    return (
        un.reshape(1, ru_rows, width), in_.reshape(ri_rows, 1, width),
        ub.reshape(1, ru_rows, width), ib.reshape(ri_rows, 1, width),
        grads.reshape(1, 1, slots, size, size),
    )


def solution(mesh):
    body = functools.partial(shards, mesh.shape["urow"], mesh.shape["icol"])
    row = P("urow", "icol", None)
    return jax.shard_map(
        body,
        mesh=mesh,
        in_specs=(row, row, row, row, row, row, P("urow", "icol"), P("urow", "icol", None, None, None)),
        out_specs=(row, row, row, row, P("urow", "icol", None, None, None)),
        check_vma=False,
    )
```
